32 devices in a mesh: frames: 16 (over z, y, core), tblk: 2 (over x).
Axes of the slice: x: 2, y: 2, z: 4, core: 2. Of those that a mesh axis runs over, the one named last changes fastest.
Arguments:
- momentum: bfloat16 [2, 16, 3, 128, 128, 128], P('tblk', 'frames'), may hold values from -6 to 6
- mode_list: int32 [2048], replicated, may hold values from 2113 to 137312, as said below
Outputs:
- correlation: float32 [2, 16, 2048], P('tblk', None, 'frames')
- strength: float32 [2, 2048], P('tblk', 'frames')
The draws below stay inside these ranges and needn't reach their ends.
Inputs may be any that keep to these rules, and one draw needn't show every extreme that they name: `mode_list`: distinct encodings (kz * 65 + ky + 32) * 65 + kx + 32 of integer wavevectors with kx^2 + ky^2 + kz^2 <= 32^2 in the upper half space (kz > 0, or kz = 0 and ky > 0, or kz = ky = 0 and kx > 0). Owner o along frames owns entries o * 128 to (o + 1) * 128 - 1.
All inputs are finite; a program needn't handle non-finite values.
Results may differ from the reference program's by a relative error of at most 0.0012.
Values sent between devices are 32-bit elements; how exact they have to be, the bound alone decides.
A program may use at most 192 MiB of HBM per device.

```python
import math
import jax
import jax.numpy as jnp
from jax import lax

GRID = 128
KMAX = 32
BLOCKS = 2
BLK_FRAMES = 16
FRAMES = 32
LAGS = 16
MODES = 2048


def draw_mode_list(key, part):
    side_len = 2 * KMAX + 1
    grid_count = (KMAX + 1) * side_len * side_len
    flat_index = jnp.arange(grid_count, dtype=jnp.int32)
    z_freq = flat_index // (side_len * side_len)
    y_freq = flat_index // side_len % side_len - KMAX
    x_freq = flat_index % side_len - KMAX
    radius = x_freq * x_freq + y_freq * y_freq + z_freq * z_freq
    upper_half = (z_freq > 0) | (z_freq == 0) & (y_freq > 0) | (z_freq == 0) & (y_freq == 0) & (x_freq > 0)
    in_shell = upper_half & (radius <= KMAX * KMAX)
    lowest_idx = KMAX * side_len + KMAX + 1
    topmost_idx = (KMAX * side_len + KMAX) * side_len + KMAX
    random_part = jax.random.randint(key, (grid_count,), 0, 4096, dtype=jnp.int32)
    scores = jnp.where(in_shell, random_part * 262144 + flat_index, -1 - flat_index)
    forced = (flat_index == lowest_idx) | (flat_index == topmost_idx)
    scores = jnp.where(forced, 1073741824 + flat_index, scores)
    chosen = lax.top_k(scores, MODES)[1]
    return chosen.astype(jnp.int32)


def block_levels(rng, shape, cuts, low, largest):
    def one(axis_at, shards_of):
        heights = jax.random.uniform(jax.random.fold_in(jax.random.fold_in(rng, 6), axis_at), (shards_of,), jnp.float32, low / len(cuts), largest / len(cuts))
        return jnp.repeat(jnp.exp(heights), shape[axis_at] // shards_of).reshape((-1,) + (1,) * (len(shape) - axis_at - 1))

    level = one(*cuts[0])
    for cut in cuts[1:]:
        level = level * one(*cut)
    return level


def scatter_about(own_key, dims, width, bound, pieces=(), kind=jnp.bfloat16):
    array = width * jax.random.normal(own_key, dims, jnp.float32)
    if pieces:
        array = array * block_levels(own_key, dims, pieces, -0.22, 0.18)
    return jnp.clip(array, -bound, bound).astype(kind)


def setup_inputs(seed: int = 0) -> dict:
    keys = jax.random.split(jax.random.key(seed), 3)
    momentum = scatter_about(keys[0], (BLOCKS, BLK_FRAMES, 3, GRID, GRID, GRID), 1.0, 6.0, ((0, 2), (1, 16)))
    mode_list = draw_mode_list(jax.random.fold_in(keys[2], 71), 0)
    return dict(momentum=momentum, mode_list=mode_list)


highest = lax.Precision.HIGHEST


def tables(length, lowest, topmost):
    position = jnp.arange(length, dtype=jnp.int32)
    frequency = jnp.arange(lowest, topmost + 1, dtype=jnp.int32)
    turn_count = jnp.mod(position[:, None] * frequency[None, :], length).astype(jnp.float32)
    angles = turn_count * (2.0 * math.pi / length)
    return jnp.cos(angles), jnp.sin(angles)


def transform(frame_data):
    cos_z, sin_z = tables(GRID, 0, KMAX)
    table_z = jnp.concatenate([cos_z, -sin_z], axis=1).astype(jnp.bfloat16)
    half_z = jnp.dot(frame_data.reshape(3 * GRID * GRID, GRID), table_z, preferred_element_type=jnp.float32)
    half_z = half_z.reshape(3, GRID, GRID, 2 * KMAX + 2)
    real_z = half_z[..., :KMAX + 1]
    imag_z = half_z[..., KMAX + 1:]
    cos_w, sin_w = tables(GRID, -KMAX, KMAX)
    real_y = jnp.einsum('cxyk,yq->cxqk', real_z, cos_w, precision=highest) + jnp.einsum('cxyk,yq->cxqk', imag_z, sin_w, precision=highest)
    imag_y = jnp.einsum('cxyk,yq->cxqk', imag_z, cos_w, precision=highest) - jnp.einsum('cxyk,yq->cxqk', real_z, sin_w, precision=highest)
    real_x = jnp.einsum('cxqk,xp->cpqk', real_y, cos_w, precision=highest) + jnp.einsum('cxqk,xp->cpqk', imag_y, sin_w, precision=highest)
    imag_x = jnp.einsum('cxqk,xp->cpqk', imag_y, cos_w, precision=highest) - jnp.einsum('cxqk,xp->cpqk', real_y, sin_w, precision=highest)
    spectrum = jnp.stack([real_x, imag_x]).transpose(0, 1, 4, 3, 2)
    side_len = 2 * KMAX + 1
    return spectrum.reshape(6, (KMAX + 1) * side_len * side_len) * (GRID ** -1.5)


def wave_vectors(mode_list):
    side_len = 2 * KMAX + 1
    z_freq = mode_list // (side_len * side_len)
    y_freq = (mode_list // side_len) % side_len - KMAX
    x_freq = mode_list % side_len - KMAX
    return jnp.stack([x_freq, y_freq, z_freq]).astype(jnp.float32)


def reference(momentum, mode_list):
    all_frames = momentum.reshape(FRAMES, 3, GRID, GRID, GRID)

    def per_frame(frame_data):
        return transform(frame_data)[:, mode_list]

    current = lax.map(per_frame, all_frames)
    wave_vec = wave_vectors(mode_list)
    wave_sq = jnp.sum(wave_vec * wave_vec, axis=0)

    def project(channel_part):
        along_k = jnp.sum(wave_vec[None] * channel_part, axis=1, keepdims=True)
        return channel_part - wave_vec[None] * along_k / wave_sq[None, None]

    transverse = jnp.concatenate([project(current[:, :3]), project(current[:, 3:])], axis=1)
    padded = jnp.concatenate([transverse, jnp.zeros((LAGS - 1, 6, MODES), jnp.float32)], axis=0)

    def lag_sum(lag_index):
        later_frames = lax.dynamic_slice_in_dim(padded, lag_index, FRAMES, 0)
        products = jnp.sum(transverse * later_frames, axis=1)
        return jnp.sum(products.reshape(BLOCKS, BLK_FRAMES, MODES), axis=1)

    lag_sums = lax.map(lag_sum, jnp.arange(LAGS, dtype=jnp.int32))
    lag_values = jnp.arange(LAGS, dtype=jnp.float32)
    block_ids = jnp.arange(BLOCKS, dtype=jnp.int32)
    pair_count = jnp.where(block_ids[None, :] == BLOCKS - 1, BLK_FRAMES - lag_values[:, None], jnp.float32(BLK_FRAMES))
    lagged = (lag_sums / pair_count[:, :, None]).transpose(1, 0, 2)
    strength = lagged[:, 0, :]
    correlation = lagged / (strength[:, None, :] + 1e-6)
    return correlation, strength
```

```python
import functools

import jax
import jax.numpy as jnp
import ml_dtypes
import numpy as np
from jax import lax
from jax.experimental import pallas as pl
from jax.experimental.pallas import tpu as pltpu
from jax.sharding import PartitionSpec as P

KMAX = 32
LAG_MAX = 64
HALF = KMAX + 1
SIDE = 2 * KMAX + 1
PITCH = -(-HALF // 4) * 4
ROWS = -(-SIDE // 8) * 8
CHANNELS = 8
LANES = 128
LANE_BITS = 7

f32 = jnp.float32
bf16 = jnp.bfloat16
MESH = pl.DeviceIdType.MESH


def split_table(table):
    high = table.astype(np.float32).astype(ml_dtypes.bfloat16)
    low = (table - high.astype(np.float64)).astype(np.float32).astype(ml_dtypes.bfloat16)
    return high, low


def angles(length, frequency):
    turns = np.mod(np.outer(frequency, np.arange(length)), length)
    return turns * (2.0 * np.pi / length)


def y_table(length):
    theta = angles(length, np.arange(HALF))
    table = np.zeros((2 * PITCH, length))
    table[:HALF] = np.cos(theta)
    table[PITCH : PITCH + HALF] = np.sin(theta)
    return np.concatenate(split_table(table), axis=1)


def x_table(length):
    theta = angles(length, np.arange(-KMAX, KMAX + 1))
    table = np.zeros((2 * ROWS, 2 * length))
    table[:SIDE, :length] = np.cos(theta)
    table[:SIDE, length:] = -np.sin(theta)
    table[ROWS : ROWS + SIDE, :length] = -np.sin(theta)
    table[ROWS : ROWS + SIDE, length:] = -np.cos(theta)
    return split_table(table)


def z_table(length):
    theta = angles(length, np.arange(-KMAX, KMAX + 1))
    cos_z = np.cos(theta).astype(np.float32).astype(ml_dtypes.bfloat16).astype(np.float32)
    sin_z = (-np.sin(theta)).astype(np.float32).astype(ml_dtypes.bfloat16).astype(np.float32)
    half = CHANNELS // 2
    return np.stack([cos_z] * CHANNELS + [-sin_z] * half + [sin_z] * half, axis=1)


def decode(mode_list):
    entry = mode_list.astype(f32)
    z_freq = jnp.floor((entry + 0.5) * f32(1.0 / (SIDE * SIDE)))
    rest = entry - z_freq * f32(SIDE * SIDE)
    y_index = jnp.floor((rest + 0.5) * f32(1.0 / SIDE))
    x_freq = rest - y_index * f32(SIDE) - f32(KMAX)
    return x_freq, y_index - f32(KMAX), z_freq


def modes_kernel(
    data_hbm, list_ref, ty_ref, txh_ref, txl_ref, tz_ref, out_ref,
    data, along_y, plane, index_vmem, index_smem, data_sem, index_sem,
):
    comps, grid_len, _, _ = data_hbm.shape
    owners = list_ref.shape[0]
    chunk = 16
    chunks = grid_len // chunk

    def fetch(comp, part):
        rows = pl.ds(part * chunk, chunk)
        return pltpu.make_async_copy(
            data_hbm.at[comp, rows], data.at[comp, rows], data_sem.at[comp, part]
        )

    for comp in range(comps):
        for part in range(chunks):
            fetch(comp, part).start()

    x_freq, y_freq, z_freq = decode(list_ref[...])
    sign = jnp.where(y_freq < 0, f32(-1), f32(1))
    pair = sign * y_freq * f32(ROWS) + sign * x_freq + f32(KMAX)
    index_vmem[...] = (pair * f32(LANES) + sign * z_freq + f32(KMAX)).astype(jnp.int32)
    to_smem = pltpu.make_async_copy(index_vmem, index_smem, index_sem)
    to_smem.start()

    table_y = ty_ref[...]
    table_xh = txh_ref[...]
    table_xl = txl_ref[...]
    for comp in range(comps):

        @pl.loop(0, chunks)
        def _(part):
            fetch(comp, part).wait()
            for step in range(0, chunk, 2):
                x_at = part * chunk + step
                both = jnp.concatenate([data[comp, x_at], data[comp, x_at + 1]], axis=1)
                res = jnp.dot(
                    table_y, jnp.concatenate([both, both], axis=0), preferred_element_type=f32
                )
                first = pl.multiple_of(x_at * 2 * PITCH, 8)
                along_y[pl.ds(first, 2 * PITCH), :] = res[:, :LANES]
                second = pl.multiple_of((x_at + 1) * 2 * PITCH, 8)
                along_y[pl.ds(second, 2 * PITCH), :] = res[:, LANES:]

        @pl.loop(0, (HALF + 1) // 2)
        def _(pair_at):
            ky = pair_at * 2

            def take(row):
                return along_y[pl.ds(row, grid_len, stride=2 * PITCH), :]

            cos_part = jnp.concatenate([take(ky), take(ky + 1)], axis=1)
            sin_part = jnp.concatenate([take(PITCH + ky), take(PITCH + ky + 1)], axis=1)
            block = jnp.concatenate([cos_part, sin_part], axis=0)
            high = block.astype(bf16)
            low = (block - high.astype(f32)).astype(bf16)
            res = jnp.dot(table_xh, high, preferred_element_type=f32)
            res = res + jnp.dot(table_xl, high, preferred_element_type=f32)
            res = res + jnp.dot(table_xh, low, preferred_element_type=f32)
            for which in range(2):
                lanes = slice(which * LANES, (which + 1) * LANES)
                base = (ky + which) * ROWS * CHANNELS + comp
                plane[pl.ds(base, ROWS, stride=CHANNELS), :] = res[:ROWS, lanes]
                plane[pl.ds(base + CHANNELS // 2, ROWS, stride=CHANNELS), :] = res[ROWS:, lanes]

    to_smem.wait()
    lane = lax.broadcasted_iota(jnp.int32, (CHANNELS, LANES), 1)
    row = lax.broadcasted_iota(jnp.int32, (CHANNELS, LANES), 0)
    bits = [1 << level for level in range(LANE_BITS)]
    odd = [(lane & bit) != 0 for bit in bits]
    upper = row < CHANNELS // 2
    scale = f32(float(grid_len) ** -1.5)

    @pl.loop(0, owners)
    def _(owner):
        def leaf(mode):
            code = index_smem[owner, mode]
            pair_at = pl.multiple_of((code >> LANE_BITS) * CHANNELS, CHANNELS)
            freq = code & (LANES - 1)
            value = plane[pl.ds(pair_at, CHANNELS), :]
            swapped = pltpu.roll(value, CHANNELS // 2, 0)
            return value * tz_ref[freq, :CHANNELS] + swapped * tz_ref[freq, CHANNELS:]

        def tree(start, level):
            if level < 0:
                return leaf(start)
            left = tree(start, level - 1)
            right = tree(start + bits[level], level - 1)
            kept = jnp.where(odd[level], right, left)
            moved = jnp.where(odd[level], left, right)
            return kept + pltpu.roll(moved, bits[level], 1)

        total = tree(0, len(bits) - 1)
        current = jnp.where((row & 3) == 3, f32(0), total) * scale
        x_f, y_f, z_f = decode(list_ref[pl.ds(owner, 1), :])
        wave = jnp.where((row & 3) == 0, x_f, jnp.where((row & 3) == 1, y_f, z_f))
        wave_sq = x_f * x_f + y_f * y_f + z_f * z_f
        along = current * wave
        real_dot = jnp.sum(jnp.where(upper, along, f32(0)), axis=0, keepdims=True)
        imag_dot = jnp.sum(jnp.where(upper, f32(0), along), axis=0, keepdims=True)
        removed = wave * (jnp.where(upper, real_dot, imag_dot) / wave_sq)
        out_ref[owner] = current - jnp.where((row & 3) == 3, f32(0), removed)


def frame_modes(frame, mode_rows):
    comps, grid_len = frame.shape[:2]
    owners = mode_rows.shape[0]
    table_xh, table_xl = x_table(grid_len)
    vmem = pl.BlockSpec(memory_space=pltpu.VMEM)
    chunks = grid_len // 16
    return pl.pallas_call(
        modes_kernel,
        out_shape=jax.ShapeDtypeStruct((owners, CHANNELS, LANES), f32),
        in_specs=[pl.BlockSpec(memory_space=pl.ANY)] + [vmem] * 5,
        out_specs=vmem,
        scratch_shapes=[
            pltpu.VMEM(frame.shape, bf16),
            pltpu.VMEM((grid_len * 2 * PITCH, LANES), f32),
            pltpu.VMEM(((HALF + 1) * ROWS * CHANNELS, LANES), f32),
            pltpu.VMEM((owners, LANES), jnp.int32),
            pltpu.SMEM((owners, LANES), jnp.int32),
            pltpu.SemaphoreType.DMA((comps, chunks)),
            pltpu.SemaphoreType.DMA,
        ],
        compiler_params=pltpu.CompilerParams(vmem_limit_bytes=48 * 1024 * 1024),
        name="frame_modes",
    )(
        frame,
        mode_rows,
        jnp.asarray(y_table(grid_len)),
        jnp.asarray(table_xh),
        jnp.asarray(table_xl),
        jnp.asarray(z_table(grid_len)),
    )


def lag_kernel(frames, blocks, lags, packet, corr_ref, strength_ref, held, send_sem, late_sem, recv_sem):
    me = lax.axis_index("frames")
    block = lax.axis_index("tblk")
    tail = lags - 1
    has_earlier = block > 0
    has_later = block < blocks - 1
    sends_back = jnp.logical_and(has_earlier, me < tail)
    barrier = pltpu.get_barrier_semaphore()

    def others(action):
        @pl.loop(1, frames)
        def _(step):
            action(lax.rem(me + step, frames))

    def greet(frame, in_block):
        pl.semaphore_signal(
            barrier, inc=1, device_id={"frames": frame, "tblk": in_block}, device_id_type=MESH
        )

    others(lambda frame: greet(frame, block))

    @pl.when(has_later)
    def _():
        @pl.loop(0, min(tail, frames))
        def _(frame):
            greet(frame, block + 1)

    pl.semaphore_wait(barrier, frames - 1 + jnp.where(sends_back, frames, 0))

    def within(owner):
        return pltpu.make_async_remote_copy(
            src_ref=packet.at[owner],
            dst_ref=held.at[me],
            send_sem=send_sem.at[owner],
            recv_sem=recv_sem.at[me],
            device_id={"frames": owner, "tblk": block},
            device_id_type=MESH,
        )

    def backward(owner):
        return pltpu.make_async_remote_copy(
            src_ref=packet.at[owner],
            dst_ref=held.at[frames + me],
            send_sem=late_sem.at[owner],
            recv_sem=recv_sem.at[frames + me],
            device_id={"frames": owner, "tblk": block - 1},
            device_id_type=MESH,
        )

    def arrival(slot):
        return pltpu.make_async_remote_copy(
            src_ref=held.at[slot],
            dst_ref=held.at[slot],
            send_sem=send_sem.at[0],
            recv_sem=recv_sem.at[slot],
            device_id={"frames": me, "tblk": block},
            device_id_type=MESH,
        )

    @pl.when(sends_back)
    def _():
        @pl.loop(0, frames)
        def _(step):
            backward(lax.rem(me + step, frames)).start()

    others(lambda owner: within(owner).start())
    held[me] = packet[me]

    @pl.when(jnp.logical_not(has_later))
    def _():
        held[pl.ds(frames, lags)] = jnp.zeros((lags,) + held.shape[1:], f32)

    others(lambda frame: arrival(frame).wait_recv())

    @pl.when(has_later)
    def _():
        held[frames + tail] = jnp.zeros(held.shape[1:], f32)

        @pl.loop(0, tail)
        def _(frame):
            arrival(frames + frame).wait_recv()

    anchors = held[pl.ds(0, frames)]

    def lagged(tau, missing):
        products = jnp.sum(anchors * held[pl.ds(tau, frames)], axis=0)
        total = jnp.sum(products, axis=0, keepdims=True)
        whole = f32(frames)
        return total / jnp.where(has_later, whole, whole - missing)

    strength = lagged(0, f32(0))
    strength_ref[...] = strength

    @pl.loop(0, lags)
    def _(tau):
        corr_ref[pl.ds(tau, 1), :] = lagged(tau, tau.astype(f32)) / (strength + f32(1e-06))

    others(lambda owner: within(owner).wait_send())

    @pl.when(sends_back)
    def _():
        @pl.loop(0, frames)
        def _(owner):
            backward(owner).wait_send()


def on_device(momentum, mode_list):
    frame = momentum[0, 0]
    frames = lax.axis_size("frames")
    blocks = lax.axis_size("tblk")
    lags = min(LAG_MAX, frames)
    packet = frame_modes(frame, mode_list.reshape(frames, LANES))
    vmem = pl.BlockSpec(memory_space=pltpu.VMEM)
    correlation, strength = pl.pallas_call(
        functools.partial(lag_kernel, frames, blocks, lags),
        out_shape=(
            jax.ShapeDtypeStruct((lags, LANES), f32),
            jax.ShapeDtypeStruct((1, LANES), f32),
        ),
        in_specs=[vmem],
        out_specs=(vmem, vmem),
        scratch_shapes=[
            pltpu.VMEM((frames + lags, CHANNELS, LANES), f32),
            pltpu.SemaphoreType.DMA((frames,)),
            pltpu.SemaphoreType.DMA((frames,)),
            pltpu.SemaphoreType.DMA((frames + lags,)),
        ],
        compiler_params=pltpu.CompilerParams(collective_id=0, has_side_effects=True),
        name="exchange_and_lags",
    )(packet)
    return correlation[None], strength


def solution(mesh):
    placed = (P("tblk", "frames", None, None, None, None), P())
    return jax.shard_map(
        on_device,
        mesh=mesh,
        in_specs=placed,
        out_specs=(P("tblk", None, "frames"), P("tblk", "frames")),
        check_vma=False,
    )
```

```python
import functools

import jax
import jax.numpy as jnp
import ml_dtypes
import numpy as np
from jax import lax
from jax.experimental import pallas as pl
from jax.experimental.pallas import tpu as pltpu
from jax.sharding import PartitionSpec as P

KMAX = 32
LAG_MAX = 64
HALF = KMAX + 1
SIDE = 2 * KMAX + 1
PITCH = -(-HALF // 4) * 4
ROWS = -(-SIDE // 8) * 8
CHANNELS = 8
LANES = 128
LANE_BITS = 7
DIVIDE_BITS = 19

f32 = jnp.float32
bf16 = jnp.bfloat16
MESH = pl.DeviceIdType.MESH


def split_table(table):
    high = table.astype(np.float32).astype(ml_dtypes.bfloat16)
    low = (table - high.astype(np.float64)).astype(np.float32).astype(ml_dtypes.bfloat16)
    return high, low


def angles(length, frequency):
    turns = np.mod(np.outer(frequency, np.arange(length)), length)
    return turns * (2.0 * np.pi / length)


def y_table(length):
    theta = angles(length, np.arange(HALF))
    table = np.zeros((2 * PITCH, length))
    table[:HALF] = np.cos(theta)
    table[PITCH : PITCH + HALF] = np.sin(theta)
    return np.concatenate(split_table(table), axis=0)


def x_table(length):
    theta = angles(length, np.arange(-KMAX, KMAX + 1))
    table = np.zeros((2 * ROWS, 2 * length))
    table[:SIDE, :length] = np.cos(theta)
    table[:SIDE, length:] = -np.sin(theta)
    table[ROWS : ROWS + SIDE, :length] = -np.sin(theta)
    table[ROWS : ROWS + SIDE, length:] = -np.cos(theta)
    both = np.concatenate(split_table(table), axis=0)
    return np.stack([both[:, :length], both[:, length:]])


def z_table(length):
    theta = angles(length, np.arange(-KMAX, KMAX + 1))
    cos_z = np.cos(theta).astype(np.float32).astype(ml_dtypes.bfloat16).astype(np.float32)
    sin_z = (-np.sin(theta)).astype(np.float32).astype(ml_dtypes.bfloat16).astype(np.float32)
    half = CHANNELS // 2
    return np.stack([cos_z] * CHANNELS + [-sin_z] * half + [sin_z] * half, axis=1)


def by_side(value):
    return (value * (-(-(1 << DIVIDE_BITS) // SIDE))) >> DIVIDE_BITS


def decode(mode_list):
    rest = by_side(mode_list)
    z_freq = by_side(rest)
    return mode_list - rest * SIDE - KMAX, rest - z_freq * SIDE - KMAX, z_freq


def program_kernel(
    frames, blocks, lags, frame_hbm, list_hbm, ty_hbm, tx_hbm, tz_hbm, lagged_ref,
    data, mode_rows, ty_ref, tx_ref, tz_ref, along_y, plane, place_vmem, place_smem,
    freq_vmem, freq_smem, packet, held, data_sem, table_sem, place_sem,
    send_sem, late_sem, recv_sem,
):
    comps, grid_len, _, _ = frame_hbm.shape
    chunk = 16
    chunks = grid_len // chunk
    me = lax.axis_index("frames")
    block = lax.axis_index("tblk")
    tail = lags - 1
    has_later = block < blocks - 1
    sends_back = jnp.logical_and(block > 0, me < tail)
    barrier = pltpu.get_barrier_semaphore()

    def fetch(comp, part):
        rows = pl.ds(part * chunk, chunk)
        return pltpu.make_async_copy(
            frame_hbm.at[comp, rows], data.at[comp, rows], data_sem.at[comp, part]
        )

    list_in = pltpu.make_async_copy(list_hbm, mode_rows, table_sem.at[0])
    ty_in = pltpu.make_async_copy(ty_hbm, ty_ref, table_sem.at[1])
    tx_in = pltpu.make_async_copy(tx_hbm, tx_ref, table_sem.at[2])
    tz_in = pltpu.make_async_copy(tz_hbm, tz_ref, table_sem.at[3])
    ty_in.start()
    list_in.start()
    for comp in range(comps):
        for part in range(chunks):
            fetch(comp, part).start()
        if comp == 0:
            tx_in.start()
    tz_in.start()

    def greet(frame, in_block):
        pl.semaphore_signal(
            barrier, inc=1, device_id={"frames": frame, "tblk": in_block}, device_id_type=MESH
        )

    @pl.loop(1, frames)
    def _(step):
        greet(lax.rem(me + step, frames), block)

    @pl.when(has_later)
    def _():
        @pl.loop(0, tail)
        def _(frame):
            greet(frame, block + 1)

    list_in.wait()
    x_freq, y_freq, z_freq = decode(mode_rows[...])
    sign = jnp.where(y_freq < 0, -1, 1)
    place_vmem[...] = sign * (y_freq * ROWS + x_freq) + KMAX
    freq_vmem[...] = sign * z_freq + KMAX
    place_out = pltpu.make_async_copy(place_vmem, place_smem, place_sem.at[0])
    freq_out = pltpu.make_async_copy(freq_vmem, freq_smem, place_sem.at[1])
    place_out.start()
    freq_out.start()

    ty_in.wait()
    table_y = ty_ref[...]
    for comp in range(comps):

        @pl.loop(0, chunks)
        def _(part):
            fetch(comp, part).wait()
            for step in range(0, chunk, 2):
                x_at = part * chunk + step
                both = jnp.concatenate([data[comp, x_at], data[comp, x_at + 1]], axis=1)
                res = jnp.dot(table_y, both, preferred_element_type=f32)
                res = res[: 2 * PITCH] + res[2 * PITCH :]
                first = pl.multiple_of(x_at * 2 * PITCH, 8)
                along_y[pl.ds(first, 2 * PITCH), :] = res[:, :LANES]
                second = pl.multiple_of((x_at + 1) * 2 * PITCH, 8)
                along_y[pl.ds(second, 2 * PITCH), :] = res[:, LANES:]

        if comp == 0:
            tx_in.wait()

        @pl.loop(0, (HALF + 1) // 2)
        def _(pair_at):
            ky = pair_at * 2

            def take(row):
                return along_y[pl.ds(row, grid_len, stride=2 * PITCH), :]

            cos_part = jnp.concatenate([take(ky), take(ky + 1)], axis=1)
            sin_part = jnp.concatenate([take(PITCH + ky), take(PITCH + ky + 1)], axis=1)
            values = jnp.concatenate([cos_part, sin_part], axis=0)
            high = values.astype(bf16)
            low = (values - high.astype(f32)).astype(bf16)
            table_x = jnp.concatenate([tx_ref[0], tx_ref[1]], axis=1)
            res = jnp.dot(table_x, high, preferred_element_type=f32)
            res_low = jnp.dot(table_x[: 2 * ROWS], low, preferred_element_type=f32)
            res = res[: 2 * ROWS] + res[2 * ROWS :] + res_low
            half = CHANNELS // 2
            for which in range(2):
                lanes = slice(which * LANES, (which + 1) * LANES)
                base = (ky + which) * ROWS * 2 * CHANNELS + comp
                real, imag = res[:ROWS, lanes], res[ROWS:, lanes]
                for at, value in enumerate((real, imag, imag, real)):
                    plane[pl.ds(base + at * half, ROWS, stride=2 * CHANNELS), :] = value

    place_out.wait()
    freq_out.wait()
    tz_in.wait()
    pl.semaphore_wait(barrier, frames - 1 + jnp.where(sends_back, frames, 0))

    def within(owner):
        return pltpu.make_async_remote_copy(
            src_ref=packet.at[owner],
            dst_ref=held.at[me],
            send_sem=send_sem.at[owner],
            recv_sem=recv_sem.at[me],
            device_id={"frames": owner, "tblk": block},
            device_id_type=MESH,
        )

    def backward(owner):
        return pltpu.make_async_remote_copy(
            src_ref=packet.at[owner],
            dst_ref=held.at[frames + me],
            send_sem=late_sem.at[owner],
            recv_sem=recv_sem.at[frames + me],
            device_id={"frames": owner, "tblk": block - 1},
            device_id_type=MESH,
        )

    def arrival(slot):
        return pltpu.make_async_remote_copy(
            src_ref=held.at[slot],
            dst_ref=held.at[slot],
            send_sem=send_sem.at[0],
            recv_sem=recv_sem.at[slot],
            device_id={"frames": me, "tblk": block},
            device_id_type=MESH,
        )

    lane = lax.broadcasted_iota(jnp.int32, (CHANNELS, LANES), 1)
    row = lax.broadcasted_iota(jnp.int32, (CHANNELS, LANES), 0)
    bits = [1 << level for level in range(LANE_BITS)]
    odd = [(lane & bit) != 0 for bit in bits]
    upper = row < CHANNELS // 2
    used = (row & 3) != 3
    scale = f32(float(grid_len) ** -1.5)

    @pl.loop(0, frames)
    def _(step):
        owner = lax.rem(me + step, frames)

        def leaf(mode):
            place = place_smem[owner, mode] * (2 * CHANNELS)
            freq = freq_smem[owner, mode]
            value = plane[pl.ds(place, 2 * CHANNELS), :] * tz_ref[freq]
            return value[:CHANNELS] + value[CHANNELS:]

        def tree(start, level):
            if level < 0:
                return leaf(start)
            left = tree(start, level - 1)
            right = tree(start + bits[level], level - 1)
            kept = jnp.where(odd[level], right, left)
            moved = jnp.where(odd[level], left, right)
            return kept + pltpu.roll(moved, bits[level], 1)

        total = tree(0, len(bits) - 1)
        current = jnp.where(used, total, f32(0)) * scale
        x_f, y_f, z_f = (k.astype(f32) for k in decode(mode_rows[pl.ds(owner, 1), :]))
        wave = jnp.where((row & 3) == 0, x_f, jnp.where((row & 3) == 1, y_f, z_f))
        wave_sq = x_f * x_f + y_f * y_f + z_f * z_f
        along = current * wave
        real_dot = jnp.sum(jnp.where(upper, along, f32(0)), axis=0, keepdims=True)
        imag_dot = jnp.sum(jnp.where(upper, f32(0), along), axis=0, keepdims=True)
        removed = wave * (jnp.where(upper, real_dot, imag_dot) / wave_sq)
        transverse = current - jnp.where(used, removed, f32(0))
        packet[owner] = transverse

        @pl.when(sends_back)
        def _():
            backward(owner).start()

        @pl.when(step > 0)
        def _():
            within(owner).start()

        @pl.when(step == 0)
        def _():
            held[me] = transverse

    @pl.when(jnp.logical_not(has_later))
    def _():
        held[pl.ds(frames, lags)] = jnp.zeros((lags,) + held.shape[1:], f32)

    @pl.loop(1, frames)
    def _(step):
        arrival(lax.rem(me + step, frames)).wait_recv()

    @pl.when(has_later)
    def _():
        held[frames + tail] = jnp.zeros(held.shape[1:], f32)

        @pl.loop(0, tail)
        def _(frame):
            arrival(frames + frame).wait_recv()

    anchors = held[pl.ds(0, frames)]

    @pl.loop(0, lags)
    def _(tau):
        products = jnp.sum(anchors * held[pl.ds(tau, frames)], axis=0)
        total = jnp.sum(products, axis=0, keepdims=True)
        whole = f32(frames)
        pairs = jnp.where(has_later, whole, whole - tau.astype(f32))
        lagged_ref[pl.ds(tau, 1), :] = total / pairs

    @pl.loop(1, frames)
    def _(step):
        within(lax.rem(me + step, frames)).wait_send()

    @pl.when(sends_back)
    def _():
        @pl.loop(0, frames)
        def _(owner):
            backward(owner).wait_send()


def on_device(momentum, mode_list):
    frame = momentum[0, 0]
    comps, grid_len = frame.shape[:2]
    frames = lax.axis_size("frames")
    blocks = lax.axis_size("tblk")
    lags = min(LAG_MAX, frames)
    mode_rows = mode_list.reshape(frames, LANES)
    tables = [y_table(grid_len), x_table(grid_len), z_table(grid_len)]
    places = [pltpu.VMEM(mode_rows.shape, jnp.int32), pltpu.SMEM(mode_rows.shape, jnp.int32)]
    lagged = pl.pallas_call(
        functools.partial(program_kernel, frames, blocks, lags),
        out_shape=jax.ShapeDtypeStruct((lags, LANES), f32),
        in_specs=[pl.BlockSpec(memory_space=pl.ANY)] * 5,
        out_specs=pl.BlockSpec(memory_space=pltpu.VMEM),
        scratch_shapes=[pltpu.VMEM(frame.shape, bf16), pltpu.VMEM(mode_rows.shape, jnp.int32)]
        + [pltpu.VMEM(table.shape, table.dtype) for table in tables]
        + [
            pltpu.VMEM((grid_len * 2 * PITCH, LANES), f32),
            pltpu.VMEM(((HALF + 1) * ROWS * 2 * CHANNELS, LANES), f32),
        ]
        + places
        + places
        + [
            pltpu.VMEM((frames, CHANNELS, LANES), f32),
            pltpu.VMEM((frames + lags, CHANNELS, LANES), f32),
            pltpu.SemaphoreType.DMA((comps, grid_len // 16)),
            pltpu.SemaphoreType.DMA((4,)),
            pltpu.SemaphoreType.DMA((2,)),
            pltpu.SemaphoreType.DMA((frames,)),
            pltpu.SemaphoreType.DMA((frames,)),
            pltpu.SemaphoreType.DMA((frames + lags,)),
        ],
        compiler_params=pltpu.CompilerParams(
            collective_id=0, has_side_effects=True, vmem_limit_bytes=56 * 1024 * 1024
        ),
        name="modes_exchange_lags",
    )(frame, mode_rows, *[jnp.asarray(table) for table in tables])
    strength = lagged[0:1]
    return (lagged / (strength + 1e-06))[None], strength


def solution(mesh):
    placed = (P("tblk", "frames", None, None, None, None), P())
    return jax.shard_map(
        on_device,
        mesh=mesh,
        in_specs=placed,
        out_specs=(P("tblk", None, "frames"), P("tblk", "frames")),
        check_vma=False,
    )
```

```python
import functools

import jax
import jax.numpy as jnp
import ml_dtypes
import numpy as np
from jax import lax
from jax.experimental import pallas as pl
from jax.experimental.pallas import tpu as pltpu
from jax.sharding import PartitionSpec as P

KMAX = 32
LAG_MAX = 64
HALF = KMAX + 1
SIDE = 2 * KMAX + 1
PITCH = -(-HALF // 4) * 4
ROWS = -(-SIDE // 8) * 8
CHANNELS = 8
LANES = 128
LANE_BITS = 7
DIVIDE_BITS = 19

f32 = jnp.float32
bf16 = jnp.bfloat16
MESH = pl.DeviceIdType.MESH


def split_table(table):
    high = table.astype(np.float32).astype(ml_dtypes.bfloat16)
    low = (table - high.astype(np.float64)).astype(np.float32).astype(ml_dtypes.bfloat16)
    return high, low


def angles(length, frequency):
    turns = np.mod(np.outer(frequency, np.arange(length)), length)
    return turns * (2.0 * np.pi / length)


def y_table(length):
    theta = angles(length, np.arange(HALF))
    table = np.zeros((2 * PITCH, length))
    table[:HALF] = np.cos(theta)
    table[PITCH : PITCH + HALF] = np.sin(theta)
    return np.concatenate(split_table(table), axis=0)


def x_table(length):
    theta = angles(length, np.arange(-KMAX, KMAX + 1))
    table = np.zeros((2 * ROWS, 2 * length))
    table[:SIDE, :length] = np.cos(theta)
    table[:SIDE, length:] = -np.sin(theta)
    table[ROWS : ROWS + SIDE, :length] = -np.sin(theta)
    table[ROWS : ROWS + SIDE, length:] = -np.cos(theta)
    both = np.concatenate(split_table(table), axis=0)
    return np.stack([both[:, :length], both[:, length:]])


def z_table(length):
    theta = angles(length, np.arange(-KMAX, KMAX + 1))
    cos_z = np.cos(theta).astype(np.float32).astype(ml_dtypes.bfloat16).astype(np.float32)
    sin_z = (-np.sin(theta)).astype(np.float32).astype(ml_dtypes.bfloat16).astype(np.float32)
    half = CHANNELS // 2
    return np.stack([cos_z] * CHANNELS + [-sin_z] * half + [sin_z] * half, axis=1)


def by_side(value):
    return (value * (-(-(1 << DIVIDE_BITS) // SIDE))) >> DIVIDE_BITS


def decode(mode_list):
    rest = by_side(mode_list)
    z_freq = by_side(rest)
    return mode_list - rest * SIDE - KMAX, rest - z_freq * SIDE - KMAX, z_freq


def program_kernel(
    frames, blocks, lags, frame_hbm, list_hbm, ty_hbm, tx_hbm, tz_hbm, lagged_ref,
    data, mode_rows, ty_ref, tx_ref, tz_ref, along_y, plane, place_vmem, place_smem,
    freq_vmem, freq_smem, packet, held, data_sem, table_sem, place_sem,
    send_sem, late_sem, recv_sem,
):
    comps, grid_len, _, _ = frame_hbm.shape
    chunk = grid_len // data_sem.shape[1]
    chunks = grid_len // chunk
    me = lax.axis_index("frames")
    block = lax.axis_index("tblk")
    tail = lags - 1
    has_later = block < blocks - 1
    sends_back = jnp.logical_and(block > 0, me < tail)
    barrier = pltpu.get_barrier_semaphore()

    def fetch(comp, part):
        rows = pl.ds(part * chunk, chunk)
        return pltpu.make_async_copy(
            frame_hbm.at[comp, rows], data.at[comp, rows], data_sem.at[comp, part]
        )

    list_in = pltpu.make_async_copy(list_hbm, mode_rows, table_sem.at[0])
    ty_in = pltpu.make_async_copy(ty_hbm, ty_ref, table_sem.at[1])
    tx_in = pltpu.make_async_copy(tx_hbm, tx_ref, table_sem.at[2])
    tz_in = pltpu.make_async_copy(tz_hbm, tz_ref, table_sem.at[3])
    ty_in.start()
    list_in.start()
    for comp in range(comps):
        for part in range(chunks):
            fetch(comp, part).start()
            if comp == 0 and part == 0:
                tx_in.start()
    tz_in.start()

    def greet(frame, in_block):
        pl.semaphore_signal(
            barrier, inc=1, device_id={"frames": frame, "tblk": in_block}, device_id_type=MESH
        )

    @pl.loop(1, frames)
    def _(step):
        greet(lax.rem(me + step, frames), block)

    @pl.when(has_later)
    def _():
        @pl.loop(0, tail)
        def _(frame):
            greet(frame, block + 1)

    list_in.wait()
    x_freq, y_freq, z_freq = decode(mode_rows[...])
    sign = jnp.where(y_freq < 0, -1, 1)
    place_vmem[...] = sign * (y_freq * ROWS + x_freq) + KMAX
    freq_vmem[...] = sign * z_freq + KMAX
    place_out = pltpu.make_async_copy(place_vmem, place_smem, place_sem.at[0])
    freq_out = pltpu.make_async_copy(freq_vmem, freq_smem, place_sem.at[1])
    place_out.start()
    freq_out.start()

    ty_in.wait()
    tx_in.wait()
    table_y = ty_ref[...]

    @pl.loop(0, comps)
    def _(comp):
        @pl.loop(0, chunks)
        def _(part):
            fetch(comp, part).wait()
            for step in range(0, chunk, 2):
                x_at = part * chunk + step
                both = jnp.concatenate([data[comp, x_at], data[comp, x_at + 1]], axis=1)
                res = jnp.dot(table_y, both, preferred_element_type=f32)
                res = res[: 2 * PITCH] + res[2 * PITCH :]
                first = pl.multiple_of(x_at * 2 * PITCH, 8)
                along_y[pl.ds(first, 2 * PITCH), :] = res[:, :LANES]
                second = pl.multiple_of((x_at + 1) * 2 * PITCH, 8)
                along_y[pl.ds(second, 2 * PITCH), :] = res[:, LANES:]

        for ky in range(0, HALF, 2):

            def take(row):
                return along_y[pl.ds(row, grid_len, stride=2 * PITCH), :]

            cos_part = jnp.concatenate([take(ky), take(ky + 1)], axis=1)
            sin_part = jnp.concatenate([take(PITCH + ky), take(PITCH + ky + 1)], axis=1)
            values = jnp.concatenate([cos_part, sin_part], axis=0)
            high = values.astype(bf16)
            low = (values - high.astype(f32)).astype(bf16)
            table_x = jnp.concatenate([tx_ref[0], tx_ref[1]], axis=1)
            res = jnp.dot(table_x, high, preferred_element_type=f32)
            res_low = jnp.dot(table_x[: 2 * ROWS], low, preferred_element_type=f32)
            res = res[: 2 * ROWS] + res[2 * ROWS :] + res_low
            half = CHANNELS // 2
            for which in range(2):
                lanes = slice(which * LANES, (which + 1) * LANES)
                base = (ky + which) * ROWS * 2 * CHANNELS + comp
                real, imag = res[:ROWS, lanes], res[ROWS:, lanes]
                for at, value in enumerate((real, imag, imag, real)):
                    plane[pl.ds(base + at * half, ROWS, stride=2 * CHANNELS), :] = value

    place_out.wait()
    freq_out.wait()
    tz_in.wait()
    pl.semaphore_wait(barrier, frames - 1 + jnp.where(sends_back, frames, 0))

    def within(owner):
        return pltpu.make_async_remote_copy(
            src_ref=packet.at[owner],
            dst_ref=held.at[me],
            send_sem=send_sem.at[owner],
            recv_sem=recv_sem.at[me],
            device_id={"frames": owner, "tblk": block},
            device_id_type=MESH,
        )

    def backward(owner):
        return pltpu.make_async_remote_copy(
            src_ref=packet.at[owner],
            dst_ref=held.at[frames + me],
            send_sem=late_sem.at[owner],
            recv_sem=recv_sem.at[frames + me],
            device_id={"frames": owner, "tblk": block - 1},
            device_id_type=MESH,
        )

    def arrival(slot):
        return pltpu.make_async_remote_copy(
            src_ref=held.at[slot],
            dst_ref=held.at[slot],
            send_sem=send_sem.at[0],
            recv_sem=recv_sem.at[slot],
            device_id={"frames": me, "tblk": block},
            device_id_type=MESH,
        )

    lane = lax.broadcasted_iota(jnp.int32, (CHANNELS, LANES), 1)
    row = lax.broadcasted_iota(jnp.int32, (CHANNELS, LANES), 0)
    bits = [1 << level for level in range(LANE_BITS)]
    odd = [(lane & bit) != 0 for bit in bits]
    upper = row < CHANNELS // 2
    used = (row & 3) != 3
    scale = f32(float(grid_len) ** -1.5)

    def picked(owner):
        def leaf(mode):
            place = place_smem[owner, mode] * (2 * CHANNELS)
            freq = freq_smem[owner, mode]
            value = plane[pl.ds(place, 2 * CHANNELS), :] * tz_ref[freq]
            return value[:CHANNELS] + value[CHANNELS:]

        def tree(start, level):
            if level < 0:
                return leaf(start)
            left = tree(start, level - 1)
            right = tree(start + bits[level], level - 1)
            kept = jnp.where(odd[level], right, left)
            moved = jnp.where(odd[level], left, right)
            return kept + pltpu.roll(moved, bits[level], 1)

        total = tree(0, len(bits) - 1)
        current = jnp.where(used, total, f32(0)) * scale
        x_f, y_f, z_f = (k.astype(f32) for k in decode(mode_rows[pl.ds(owner, 1), :]))
        wave = jnp.where((row & 3) == 0, x_f, jnp.where((row & 3) == 1, y_f, z_f))
        wave_sq = x_f * x_f + y_f * y_f + z_f * z_f
        along = current * wave
        real_dot = jnp.sum(jnp.where(upper, along, f32(0)), axis=0, keepdims=True)
        imag_dot = jnp.sum(jnp.where(upper, f32(0), along), axis=0, keepdims=True)
        removed = wave * (jnp.where(upper, real_dot, imag_dot) / wave_sq)
        return current - jnp.where(used, removed, f32(0))

    @pl.loop(0, frames, step=2)
    def _(step):
        pair = [lax.rem(me + step + which, frames) for which in range(2)]
        transverse = [picked(owner) for owner in pair]
        for owner, value in zip(pair, transverse):
            packet[owner] = value

        @pl.when(sends_back)
        def _():
            for owner in pair:
                backward(owner).start()

        @pl.when(step > 0)
        def _():
            within(pair[0]).start()

        within(pair[1]).start()

        @pl.when(step == 0)
        def _():
            held[me] = transverse[0]

    @pl.when(jnp.logical_not(has_later))
    def _():
        held[pl.ds(frames, lags)] = jnp.zeros((lags,) + held.shape[1:], f32)

    @pl.loop(1, frames)
    def _(step):
        arrival(lax.rem(me + step, frames)).wait_recv()

    @pl.when(has_later)
    def _():
        held[frames + tail] = jnp.zeros(held.shape[1:], f32)

        @pl.loop(0, tail)
        def _(frame):
            arrival(frames + frame).wait_recv()

    anchors = held[pl.ds(0, frames)]

    @pl.loop(0, lags)
    def _(tau):
        products = jnp.sum(anchors * held[pl.ds(tau, frames)], axis=0)
        total = jnp.sum(products, axis=0, keepdims=True)
        whole = f32(frames)
        pairs = jnp.where(has_later, whole, whole - tau.astype(f32))
        lagged_ref[pl.ds(tau, 1), :] = total / pairs

    @pl.loop(1, frames)
    def _(step):
        within(lax.rem(me + step, frames)).wait_send()

    @pl.when(sends_back)
    def _():
        @pl.loop(0, frames)
        def _(owner):
            backward(owner).wait_send()


def finish_kernel(lagged_hbm, corr_ref, strength_ref, lagged_ref, sem):
    lagged_in = pltpu.make_async_copy(lagged_hbm, lagged_ref, sem)
    lagged_in.start()
    lagged_in.wait()
    lagged = lagged_ref[...]
    strength = lagged[:1]
    strength_ref[...] = strength
    corr_ref[0] = lagged / (strength + f32(1e-06))


def on_device(momentum, mode_list):
    frame = momentum[0, 0]
    comps, grid_len = frame.shape[:2]
    frames = lax.axis_size("frames")
    blocks = lax.axis_size("tblk")
    lags = min(LAG_MAX, frames)
    mode_rows = mode_list.reshape(frames, LANES)
    tables = [y_table(grid_len), x_table(grid_len), z_table(grid_len)]
    places = [pltpu.VMEM(mode_rows.shape, jnp.int32), pltpu.SMEM(mode_rows.shape, jnp.int32)]
    lagged = pl.pallas_call(
        functools.partial(program_kernel, frames, blocks, lags),
        out_shape=jax.ShapeDtypeStruct((lags, LANES), f32),
        in_specs=[pl.BlockSpec(memory_space=pl.ANY)] * 5,
        out_specs=pl.BlockSpec(memory_space=pltpu.VMEM),
        scratch_shapes=[pltpu.VMEM(frame.shape, bf16), pltpu.VMEM(mode_rows.shape, jnp.int32)]
        + [pltpu.VMEM(table.shape, table.dtype) for table in tables]
        + [
            pltpu.VMEM((grid_len * 2 * PITCH, LANES), f32),
            pltpu.VMEM(((HALF + 1) * ROWS * 2 * CHANNELS, LANES), f32),
        ]
        + places
        + places
        + [
            pltpu.VMEM((frames, CHANNELS, LANES), f32),
            pltpu.VMEM((frames + lags, CHANNELS, LANES), f32),
            pltpu.SemaphoreType.DMA((comps, 4)),
            pltpu.SemaphoreType.DMA((4,)),
            pltpu.SemaphoreType.DMA((2,)),
            pltpu.SemaphoreType.DMA((frames,)),
            pltpu.SemaphoreType.DMA((frames,)),
            pltpu.SemaphoreType.DMA((frames + lags,)),
        ],
        compiler_params=pltpu.CompilerParams(
            collective_id=0, has_side_effects=True, vmem_limit_bytes=56 * 1024 * 1024
        ),
        name="modes_exchange_lags",
    )(frame, mode_rows, *[jnp.asarray(table) for table in tables])
    return pl.pallas_call(
        finish_kernel,
        out_shape=(
            jax.ShapeDtypeStruct((1, lags, LANES), f32),
            jax.ShapeDtypeStruct((1, LANES), f32),
        ),
        in_specs=[pl.BlockSpec(memory_space=pl.ANY)],
        scratch_shapes=[pltpu.VMEM(lagged.shape, f32), pltpu.SemaphoreType.DMA],
        compiler_params=pltpu.CompilerParams(vmem_limit_bytes=56 * 1024 * 1024),
        name="correlation",
    )(lagged)


def solution(mesh):
    placed = (P("tblk", "frames", None, None, None, None), P())
    return jax.shard_map(
        on_device,
        mesh=mesh,
        in_specs=placed,
        out_specs=(P("tblk", None, "frames"), P("tblk", "frames")),
        check_vma=False,
    )
```

```python
import functools
import math

import jax
import jax.numpy as jnp
import ml_dtypes
import numpy as np
from jax import lax
from jax.experimental import pallas as pl
from jax.experimental.pallas import tpu as pltpu
from jax.sharding import PartitionSpec as P

KMAX = 32
LAG_MAX = 64
HALF = KMAX + 1
SIDE = 2 * KMAX + 1
PITCH = -(-HALF // 4) * 4
ROWS = -(-SIDE // 8) * 8
CHANNELS = 8
LANES = 128
LANE_BITS = 7
DIVIDE_BITS = 19

f32 = jnp.float32
bf16 = jnp.bfloat16
MESH = pl.DeviceIdType.MESH


def split_table(table):
    high = table.astype(np.float32).astype(ml_dtypes.bfloat16)
    low = (table - high.astype(np.float64)).astype(np.float32).astype(ml_dtypes.bfloat16)
    return high, low


def angles(length, frequency):
    turns = np.mod(np.outer(frequency, np.arange(length)), length)
    return turns * (2.0 * np.pi / length)


def y_table(length):
    theta = angles(length, np.arange(HALF))
    table = np.zeros((2 * PITCH, length))
    table[:HALF] = np.cos(theta)
    table[PITCH : PITCH + HALF] = np.sin(theta)
    return np.concatenate(split_table(table), axis=0)


def x_table(length):
    theta = angles(length, np.arange(-KMAX, KMAX + 1))
    table = np.zeros((2 * ROWS, 2 * length))
    table[:SIDE, :length] = np.cos(theta)
    table[:SIDE, length:] = -np.sin(theta)
    table[ROWS : ROWS + SIDE, :length] = -np.sin(theta)
    table[ROWS : ROWS + SIDE, length:] = -np.cos(theta)
    both = np.concatenate(split_table(table), axis=0)
    return np.stack([both[:, :length], both[:, length:]])


def z_table(length):
    theta = angles(length, np.arange(-KMAX, KMAX + 1))
    cos_z = np.cos(theta).astype(np.float32).astype(ml_dtypes.bfloat16).astype(np.float32)
    sin_z = (-np.sin(theta)).astype(np.float32).astype(ml_dtypes.bfloat16).astype(np.float32)
    half = CHANNELS // 2
    return np.stack([cos_z] * CHANNELS + [-sin_z] * half + [sin_z] * half, axis=1)


def by_side(value):
    return (value * (-(-(1 << DIVIDE_BITS) // SIDE))) >> DIVIDE_BITS


def decode(mode_list):
    rest = by_side(mode_list)
    z_freq = by_side(rest)
    return mode_list - rest * SIDE - KMAX, rest - z_freq * SIDE - KMAX, z_freq


def program_kernel(
    frames, blocks, lags, frame_hbm, list_hbm, ty_hbm, tx_hbm, tz_hbm, lagged_ref,
    data, mode_rows, ty_ref, tx_ref, tz_ref, along_y, plane, place_vmem, place_smem,
    freq_vmem, freq_smem, packet, held, data_sem, table_sem, place_sem,
    send_sem, late_sem, recv_sem,
):
    comps, grid_len, _, _ = frame_hbm.shape
    chunk = grid_len // data_sem.shape[1]
    chunks = grid_len // chunk
    me = lax.axis_index("frames")
    block = lax.axis_index("tblk")
    tail = lags - 1
    has_later = block < blocks - 1
    sends_back = jnp.logical_and(block > 0, me < tail)
    barrier = pltpu.get_barrier_semaphore()

    def fetch(comp, part):
        rows = pl.ds(part * chunk, chunk)
        return pltpu.make_async_copy(
            frame_hbm.at[comp, rows], data.at[comp, rows], data_sem.at[comp, part]
        )

    list_in = pltpu.make_async_copy(list_hbm, mode_rows, table_sem.at[0])
    ty_in = pltpu.make_async_copy(ty_hbm, ty_ref, table_sem.at[1])
    tx_in = pltpu.make_async_copy(tx_hbm, tx_ref, table_sem.at[2])
    tz_in = pltpu.make_async_copy(tz_hbm, tz_ref, table_sem.at[3])
    ty_in.start()
    list_in.start()
    for comp in range(comps):
        for part in range(chunks):
            fetch(comp, part).start()
            if comp == 0 and part == 0:
                tx_in.start()
    tz_in.start()

    def greet(frame, in_block):
        pl.semaphore_signal(
            barrier, inc=1, device_id={"frames": frame, "tblk": in_block}, device_id_type=MESH
        )

    @pl.loop(1, frames)
    def _(step):
        greet(lax.rem(me + step, frames), block)

    @pl.when(has_later)
    def _():
        @pl.loop(0, tail)
        def _(frame):
            greet(frame, block + 1)

    list_in.wait()
    x_freq, y_freq, z_freq = decode(mode_rows[...])
    sign = jnp.where(y_freq < 0, -1, 1)
    place_vmem[...] = sign * (y_freq * ROWS + x_freq) + KMAX
    freq_vmem[...] = sign * z_freq + KMAX
    place_out = pltpu.make_async_copy(place_vmem, place_smem, place_sem.at[0])
    freq_out = pltpu.make_async_copy(freq_vmem, freq_smem, place_sem.at[1])
    place_out.start()
    freq_out.start()

    ty_in.wait()
    tx_in.wait()
    table_y = ty_ref[...]

    def y_stage(comp, x_at):
        both = jnp.concatenate([data[comp, x_at], data[comp, x_at + 1]], axis=1)
        res = jnp.dot(table_y, both, preferred_element_type=f32)
        res = res[: 2 * PITCH] + res[2 * PITCH :]
        for which in range(2):
            first = (x_at + which) * 2 * PITCH
            lanes = slice(which * LANES, (which + 1) * LANES)
            along_y[comp % 2, pl.ds(first, 2 * PITCH), :] = res[:, lanes]

    def x_stage(comp, ky):
        def take(row):
            return along_y[comp % 2, pl.ds(row, grid_len, stride=2 * PITCH), :]

        cos_part = jnp.concatenate([take(ky), take(ky + 1)], axis=1)
        sin_part = jnp.concatenate([take(PITCH + ky), take(PITCH + ky + 1)], axis=1)
        values = jnp.concatenate([cos_part, sin_part], axis=0)
        high = values.astype(bf16)
        low = (values - high.astype(f32)).astype(bf16)
        table_x = jnp.concatenate([tx_ref[0], tx_ref[1]], axis=1)
        res = jnp.dot(table_x, high, preferred_element_type=f32)
        res_low = jnp.dot(table_x[: 2 * ROWS], low, preferred_element_type=f32)
        res = res[: 2 * ROWS] + res[2 * ROWS :] + res_low
        half = CHANNELS // 2
        for which in range(2):
            lanes = slice(which * LANES, (which + 1) * LANES)
            base = (ky + which) * ROWS * 2 * CHANNELS + comp
            real, imag = res[:ROWS, lanes], res[ROWS:, lanes]
            for at, value in enumerate((real, imag, imag, real)):
                plane[pl.ds(base + at * half, ROWS, stride=2 * CHANNELS), :] = value

    x_pairs = list(range(0, grid_len, 2))
    ky_pairs = list(range(0, HALF, 2))
    for part in range(chunks):
        fetch(0, part).wait()
        for x_at in range(part * chunk, (part + 1) * chunk, 2):
            y_stage(0, x_at)
    for comp in range(comps):
        ahead = x_pairs if comp + 1 < comps else []
        if ahead:
            for part in range(chunks):
                fetch(comp + 1, part).wait()
        done = 0
        for count, ky in enumerate(ky_pairs):
            x_stage(comp, ky)
            until = len(ahead) * (count + 1) // len(ky_pairs)
            for x_at in ahead[done:until]:
                y_stage(comp + 1, x_at)
            done = until

    place_out.wait()
    freq_out.wait()
    tz_in.wait()
    pl.semaphore_wait(barrier, frames - 1 + jnp.where(sends_back, frames, 0))

    def within(owner):
        return pltpu.make_async_remote_copy(
            src_ref=packet.at[owner],
            dst_ref=held.at[me],
            send_sem=send_sem.at[owner],
            recv_sem=recv_sem.at[me],
            device_id={"frames": owner, "tblk": block},
            device_id_type=MESH,
        )

    def backward(owner):
        return pltpu.make_async_remote_copy(
            src_ref=packet.at[owner],
            dst_ref=held.at[frames + me],
            send_sem=late_sem.at[owner],
            recv_sem=recv_sem.at[frames + me],
            device_id={"frames": owner, "tblk": block - 1},
            device_id_type=MESH,
        )

    def arrival(slot):
        return pltpu.make_async_remote_copy(
            src_ref=held.at[slot],
            dst_ref=held.at[slot],
            send_sem=send_sem.at[0],
            recv_sem=recv_sem.at[slot],
            device_id={"frames": me, "tblk": block},
            device_id_type=MESH,
        )

    lane = lax.broadcasted_iota(jnp.int32, (CHANNELS, LANES), 1)
    row = lax.broadcasted_iota(jnp.int32, (CHANNELS, LANES), 0)
    bits = [1 << level for level in range(LANE_BITS)]
    odd = [(lane & bit) != 0 for bit in bits]
    upper = row < CHANNELS // 2
    used = (row & 3) != 3
    scale = f32(float(grid_len) ** -1.5)

    def picked(owner):
        def leaf(mode):
            place = place_smem[owner, mode] * (2 * CHANNELS)
            freq = freq_smem[owner, mode]
            value = plane[pl.ds(place, 2 * CHANNELS), :] * tz_ref[freq]
            return value[:CHANNELS] + value[CHANNELS:]

        def tree(start, level):
            if level < 0:
                return leaf(start)
            left = tree(start, level - 1)
            right = tree(start + bits[level], level - 1)
            kept = jnp.where(odd[level], right, left)
            moved = jnp.where(odd[level], left, right)
            return kept + pltpu.roll(moved, bits[level], 1)

        total = tree(0, len(bits) - 1)
        current = jnp.where(used, total, f32(0)) * scale
        x_f, y_f, z_f = (k.astype(f32) for k in decode(mode_rows[pl.ds(owner, 1), :]))
        wave = jnp.where((row & 3) == 0, x_f, jnp.where((row & 3) == 1, y_f, z_f))
        wave_sq = x_f * x_f + y_f * y_f + z_f * z_f
        along = current * wave
        real_dot = jnp.sum(jnp.where(upper, along, f32(0)), axis=0, keepdims=True)
        imag_dot = jnp.sum(jnp.where(upper, f32(0), along), axis=0, keepdims=True)
        removed = wave * (jnp.where(upper, real_dot, imag_dot) / wave_sq)
        return current - jnp.where(used, removed, f32(0))

    group = math.gcd(frames, 4)

    @pl.loop(0, frames, step=group)
    def _(step):
        picks = [lax.rem(me + step + which, frames) for which in range(group)]
        transverse = [picked(owner) for owner in picks]
        for owner, value in zip(picks, transverse):
            packet[owner] = value

        @pl.when(sends_back)
        def _():
            for owner in picks:
                backward(owner).start()

        @pl.when(step > 0)
        def _():
            within(picks[0]).start()

        for owner in picks[1:]:
            within(owner).start()

        @pl.when(step == 0)
        def _():
            held[me] = transverse[0]

    @pl.when(jnp.logical_not(has_later))
    def _():
        held[pl.ds(frames, lags)] = jnp.zeros((lags,) + held.shape[1:], f32)

    @pl.loop(1, frames)
    def _(step):
        arrival(lax.rem(me + step, frames)).wait_recv()

    @pl.when(has_later)
    def _():
        held[frames + tail] = jnp.zeros(held.shape[1:], f32)

        @pl.loop(0, tail)
        def _(frame):
            arrival(frames + frame).wait_recv()

    anchors = held[pl.ds(0, frames)]

    def lag_rows(first):
        for tau in range(8):
            products = jnp.sum(anchors * held[pl.ds(first + tau, frames)], axis=0)
            total = jnp.sum(products, axis=0, keepdims=True)
            lagged_ref[pl.ds(first + tau, 1), :] = total
        taus = lax.broadcasted_iota(jnp.int32, (8, LANES), 0) + first
        pairs = jnp.where(has_later, frames, frames - taus).astype(f32)
        rows = pl.ds(first, 8)
        lagged_ref[rows, :] = lagged_ref[rows, :] / pairs

    @pl.loop(0, lags, step=8)
    def _(first):
        lag_rows(pl.multiple_of(first, 8))

    @pl.loop(1, frames)
    def _(step):
        within(lax.rem(me + step, frames)).wait_send()

    @pl.when(sends_back)
    def _():
        @pl.loop(0, frames)
        def _(owner):
            backward(owner).wait_send()


def finish_kernel(lagged_hbm, corr_ref, strength_ref, lagged_ref, sem):
    lagged_in = pltpu.make_async_copy(lagged_hbm, lagged_ref, sem)
    lagged_in.start()
    lagged_in.wait()
    lagged = lagged_ref[...]
    strength = lagged[:1]
    strength_ref[...] = strength
    corr_ref[0] = lagged / (strength + f32(1e-06))


def on_device(momentum, mode_list):
    frame = momentum[0, 0]
    comps, grid_len = frame.shape[:2]
    frames = lax.axis_size("frames")
    blocks = lax.axis_size("tblk")
    lags = min(LAG_MAX, frames)
    mode_rows = mode_list.reshape(frames, LANES)
    tables = [y_table(grid_len), x_table(grid_len), z_table(grid_len)]
    places = [pltpu.VMEM(mode_rows.shape, jnp.int32), pltpu.SMEM(mode_rows.shape, jnp.int32)]
    lagged = pl.pallas_call(
        functools.partial(program_kernel, frames, blocks, lags),
        out_shape=jax.ShapeDtypeStruct((lags, LANES), f32),
        in_specs=[pl.BlockSpec(memory_space=pl.ANY)] * 5,
        out_specs=pl.BlockSpec(memory_space=pltpu.VMEM),
        scratch_shapes=[pltpu.VMEM(frame.shape, bf16), pltpu.VMEM(mode_rows.shape, jnp.int32)]
        + [pltpu.VMEM(table.shape, table.dtype) for table in tables]
        + [
            pltpu.VMEM((2, grid_len * 2 * PITCH, LANES), f32),
            pltpu.VMEM(((HALF + 1) * ROWS * 2 * CHANNELS, LANES), f32),
        ]
        + places
        + places
        + [
            pltpu.VMEM((frames, CHANNELS, LANES), f32),
            pltpu.VMEM((frames + lags, CHANNELS, LANES), f32),
            pltpu.SemaphoreType.DMA((comps, 4)),
            pltpu.SemaphoreType.DMA((4,)),
            pltpu.SemaphoreType.DMA((2,)),
            pltpu.SemaphoreType.DMA((frames,)),
            pltpu.SemaphoreType.DMA((frames,)),
            pltpu.SemaphoreType.DMA((frames + lags,)),
        ],
        compiler_params=pltpu.CompilerParams(
            collective_id=0, has_side_effects=True, vmem_limit_bytes=56 * 1024 * 1024
        ),
        name="modes_exchange_lags",
    )(frame, mode_rows, *[jnp.asarray(table) for table in tables])
    return pl.pallas_call(
        finish_kernel,
        out_shape=(
            jax.ShapeDtypeStruct((1, lags, LANES), f32),
            jax.ShapeDtypeStruct((1, LANES), f32),
        ),
        in_specs=[pl.BlockSpec(memory_space=pl.ANY)],
        scratch_shapes=[pltpu.VMEM(lagged.shape, f32), pltpu.SemaphoreType.DMA],
        compiler_params=pltpu.CompilerParams(vmem_limit_bytes=56 * 1024 * 1024),
        name="correlation",
    )(lagged)


def solution(mesh):
    placed = (P("tblk", "frames", None, None, None, None), P())
    return jax.shard_map(
        on_device,
        mesh=mesh,
        in_specs=placed,
        out_specs=(P("tblk", None, "frames"), P("tblk", "frames")),
        check_vma=False,
    )
```

```python
import functools

import jax
import jax.numpy as jnp
import ml_dtypes
import numpy as np
from jax import lax
from jax.experimental import pallas as pl
from jax.experimental.pallas import tpu as pltpu
from jax.sharding import PartitionSpec as P

KMAX = 32
LAG_MAX = 64
HALF = KMAX + 1
SIDE = 2 * KMAX + 1
PITCH = -(-HALF // 4) * 4
ROWS = -(-SIDE // 8) * 8
CHANNELS = 8
LANES = 128
LANE_BITS = 7
DIVIDE_BITS = 19

f32 = jnp.float32
bf16 = jnp.bfloat16
MESH = pl.DeviceIdType.MESH


def split_table(table):
    high = table.astype(np.float32).astype(ml_dtypes.bfloat16)
    low = (table - high.astype(np.float64)).astype(np.float32).astype(ml_dtypes.bfloat16)
    return high, low


def angles(length, frequency):
    turns = np.mod(np.outer(frequency, np.arange(length)), length)
    return turns * (2.0 * np.pi / length)


def y_table(length):
    theta = angles(length, np.arange(HALF))
    table = np.zeros((2 * PITCH, length))
    table[:HALF] = np.cos(theta)
    table[PITCH : PITCH + HALF] = np.sin(theta)
    return np.concatenate(split_table(table), axis=0)


def x_table(length):
    theta = angles(length, np.arange(-KMAX, KMAX + 1))
    table = np.zeros((2 * ROWS, 2 * length))
    table[:SIDE, :length] = np.cos(theta)
    table[:SIDE, length:] = -np.sin(theta)
    table[ROWS : ROWS + SIDE, :length] = -np.sin(theta)
    table[ROWS : ROWS + SIDE, length:] = -np.cos(theta)
    both = np.concatenate(split_table(table), axis=0)
    return np.stack([both[:, :length], both[:, length:]])


def z_table(length):
    theta = angles(length, np.arange(-KMAX, KMAX + 1))
    cos_z = np.cos(theta).astype(np.float32).astype(ml_dtypes.bfloat16).astype(np.float32)
    sin_z = (-np.sin(theta)).astype(np.float32).astype(ml_dtypes.bfloat16).astype(np.float32)
    half = CHANNELS // 2
    return np.stack([cos_z] * CHANNELS + [-sin_z] * half + [sin_z] * half, axis=1)


def by_side(value):
    return (value * (-(-(1 << DIVIDE_BITS) // SIDE))) >> DIVIDE_BITS


def decode(mode_list):
    rest = by_side(mode_list)
    z_freq = by_side(rest)
    return mode_list - rest * SIDE - KMAX, rest - z_freq * SIDE - KMAX, z_freq


def program_kernel(
    frames, blocks, lags, frame_hbm, list_hbm, ty_hbm, tx_hbm, tz_hbm, lagged_ref,
    data, mode_rows, ty_ref, tx_ref, tz_ref, along_y, plane, place_vmem, place_smem,
    freq_vmem, freq_smem, packet, held, data_sem, table_sem, place_sem,
    send_sem, late_sem, recv_sem,
):
    comps, grid_len, _, _ = frame_hbm.shape
    chunk = grid_len // data_sem.shape[1]
    chunks = grid_len // chunk
    me = lax.axis_index("frames")
    block = lax.axis_index("tblk")
    tail = lags - 1
    has_later = block < blocks - 1
    sends_back = jnp.logical_and(block > 0, me < tail)
    barrier = pltpu.get_barrier_semaphore()

    def fetch(comp, part):
        rows = pl.ds(part * chunk, chunk)
        return pltpu.make_async_copy(
            frame_hbm.at[comp, rows], data.at[comp, rows], data_sem.at[comp, part]
        )

    list_in = pltpu.make_async_copy(list_hbm, mode_rows, table_sem.at[0])
    ty_in = pltpu.make_async_copy(ty_hbm, ty_ref, table_sem.at[1])
    tx_in = pltpu.make_async_copy(tx_hbm, tx_ref, table_sem.at[2])
    tz_in = pltpu.make_async_copy(tz_hbm, tz_ref, table_sem.at[3])
    ty_in.start()
    list_in.start()
    for comp in range(comps):
        for part in range(chunks):
            fetch(comp, part).start()
            if comp == 0 and part == 0:
                tx_in.start()
    tz_in.start()

    def greet(frame, in_block):
        pl.semaphore_signal(
            barrier, inc=1, device_id={"frames": frame, "tblk": in_block}, device_id_type=MESH
        )

    @pl.loop(1, frames)
    def _(step):
        greet(lax.rem(me + step, frames), block)

    @pl.when(has_later)
    def _():
        @pl.loop(0, tail)
        def _(frame):
            greet(frame, block + 1)

    list_in.wait()
    x_freq, y_freq, z_freq = decode(mode_rows[...])
    sign = jnp.where(y_freq < 0, -1, 1)
    place_vmem[...] = sign * (y_freq * ROWS + x_freq) + KMAX
    freq_vmem[...] = sign * z_freq + KMAX
    place_out = pltpu.make_async_copy(place_vmem, place_smem, place_sem.at[0])
    freq_out = pltpu.make_async_copy(freq_vmem, freq_smem, place_sem.at[1])
    place_out.start()
    freq_out.start()

    ty_in.wait()
    tx_in.wait()
    table_y = ty_ref[...]

    @pl.loop(0, comps)
    def _(comp):
        @pl.loop(0, chunks)
        def _(part):
            fetch(comp, part).wait()
            for step in range(0, chunk, 2):
                x_at = part * chunk + step
                both = jnp.concatenate([data[comp, x_at], data[comp, x_at + 1]], axis=1)
                res = jnp.dot(table_y, both, preferred_element_type=f32)
                res = res[: 2 * PITCH] + res[2 * PITCH :]
                first = pl.multiple_of(x_at * 2 * PITCH, 8)
                along_y[pl.ds(first, 2 * PITCH), :] = res[:, :LANES]
                second = pl.multiple_of((x_at + 1) * 2 * PITCH, 8)
                along_y[pl.ds(second, 2 * PITCH), :] = res[:, LANES:]

        for ky in range(0, HALF, 2):

            def take(row):
                return along_y[pl.ds(row, grid_len, stride=2 * PITCH), :]

            cos_part = jnp.concatenate([take(ky), take(ky + 1)], axis=1)
            sin_part = jnp.concatenate([take(PITCH + ky), take(PITCH + ky + 1)], axis=1)
            values = jnp.concatenate([cos_part, sin_part], axis=0)
            high = values.astype(bf16)
            low = (values - high.astype(f32)).astype(bf16)
            table_x = jnp.concatenate([tx_ref[0], tx_ref[1]], axis=1)
            res = jnp.dot(table_x, high, preferred_element_type=f32)
            res_low = jnp.dot(table_x[: 2 * ROWS], low, preferred_element_type=f32)
            res = res[: 2 * ROWS] + res[2 * ROWS :] + res_low
            half = CHANNELS // 2
            for which in range(2):
                lanes = slice(which * LANES, (which + 1) * LANES)
                base = (ky + which) * ROWS * CHANNELS + comp
                real, imag = res[:ROWS, lanes], res[ROWS:, lanes]
                for at, value in enumerate((real, imag)):
                    plane[pl.ds(base + at * half, ROWS, stride=CHANNELS), :] = value

    place_out.wait()
    freq_out.wait()
    tz_in.wait()
    pl.semaphore_wait(barrier, frames - 1 + jnp.where(sends_back, frames, 0))

    def within(owner):
        return pltpu.make_async_remote_copy(
            src_ref=packet.at[owner],
            dst_ref=held.at[me],
            send_sem=send_sem.at[owner],
            recv_sem=recv_sem.at[me],
            device_id={"frames": owner, "tblk": block},
            device_id_type=MESH,
        )

    def backward(owner):
        return pltpu.make_async_remote_copy(
            src_ref=packet.at[owner],
            dst_ref=held.at[frames + me],
            send_sem=late_sem.at[owner],
            recv_sem=recv_sem.at[frames + me],
            device_id={"frames": owner, "tblk": block - 1},
            device_id_type=MESH,
        )

    def arrival(slot):
        return pltpu.make_async_remote_copy(
            src_ref=held.at[slot],
            dst_ref=held.at[slot],
            send_sem=send_sem.at[0],
            recv_sem=recv_sem.at[slot],
            device_id={"frames": me, "tblk": block},
            device_id_type=MESH,
        )

    lane = lax.broadcasted_iota(jnp.int32, (CHANNELS, LANES), 1)
    row = lax.broadcasted_iota(jnp.int32, (CHANNELS, LANES), 0)
    bits = [1 << level for level in range(LANE_BITS)]
    odd = [(lane & bit) != 0 for bit in bits]
    upper = row < CHANNELS // 2
    used = (row & 3) != 3
    scale = f32(float(grid_len) ** -1.5)

    def picked(owner):
        def leaf(mode):
            place = place_smem[owner, mode] * CHANNELS
            freq = freq_smem[owner, mode]
            value = plane[pl.ds(place, CHANNELS), :]
            swapped = pltpu.roll(value, CHANNELS // 2, 0)
            return value * tz_ref[freq, :CHANNELS] + swapped * tz_ref[freq, CHANNELS:]

        def tree(start, level):
            if level < 0:
                return leaf(start)
            left = tree(start, level - 1)
            right = tree(start + bits[level], level - 1)
            kept = jnp.where(odd[level], right, left)
            moved = jnp.where(odd[level], left, right)
            return kept + pltpu.roll(moved, bits[level], 1)

        total = tree(0, len(bits) - 1)
        current = jnp.where(used, total, f32(0)) * scale
        x_f, y_f, z_f = (k.astype(f32) for k in decode(mode_rows[pl.ds(owner, 1), :]))
        wave = jnp.where((row & 3) == 0, x_f, jnp.where((row & 3) == 1, y_f, z_f))
        wave_sq = x_f * x_f + y_f * y_f + z_f * z_f
        along = current * wave
        real_dot = jnp.sum(jnp.where(upper, along, f32(0)), axis=0, keepdims=True)
        imag_dot = jnp.sum(jnp.where(upper, f32(0), along), axis=0, keepdims=True)
        removed = wave * (jnp.where(upper, real_dot, imag_dot) / wave_sq)
        return current - jnp.where(used, removed, f32(0))

    @pl.loop(0, frames, step=2)
    def _(step):
        pair = [lax.rem(me + step + which, frames) for which in range(2)]
        transverse = [picked(owner) for owner in pair]
        for owner, value in zip(pair, transverse):
            packet[owner] = value

        @pl.when(sends_back)
        def _():
            for owner in pair:
                backward(owner).start()

        @pl.when(step > 0)
        def _():
            within(pair[0]).start()

        within(pair[1]).start()

        @pl.when(step == 0)
        def _():
            held[me] = transverse[0]

    @pl.when(jnp.logical_not(has_later))
    def _():
        held[pl.ds(frames, lags)] = jnp.zeros((lags,) + held.shape[1:], f32)

    @pl.loop(1, frames)
    def _(step):
        arrival(lax.rem(me + step, frames)).wait_recv()

    @pl.when(has_later)
    def _():
        held[frames + tail] = jnp.zeros(held.shape[1:], f32)

        @pl.loop(0, tail)
        def _(frame):
            arrival(frames + frame).wait_recv()

    anchors = held[pl.ds(0, frames)]

    def lag_rows(first):
        for tau in range(8):
            products = jnp.sum(anchors * held[pl.ds(first + tau, frames)], axis=0)
            total = jnp.sum(products, axis=0, keepdims=True)
            lagged_ref[pl.ds(first + tau, 1), :] = total
        taus = lax.broadcasted_iota(jnp.int32, (8, LANES), 0) + first
        pairs = jnp.where(has_later, frames, frames - taus).astype(f32)
        rows = pl.ds(first, 8)
        lagged_ref[rows, :] = lagged_ref[rows, :] / pairs

    @pl.loop(0, lags, step=8)
    def _(first):
        lag_rows(pl.multiple_of(first, 8))

    @pl.loop(1, frames)
    def _(step):
        within(lax.rem(me + step, frames)).wait_send()

    @pl.when(sends_back)
    def _():
        @pl.loop(0, frames)
        def _(owner):
            backward(owner).wait_send()


def finish_kernel(lagged_hbm, corr_ref, strength_ref, lagged_ref, sem):
    lagged_in = pltpu.make_async_copy(lagged_hbm, lagged_ref, sem)
    lagged_in.start()
    lagged_in.wait()
    lagged = lagged_ref[...]
    strength = lagged[:1]
    strength_ref[...] = strength
    corr_ref[0] = lagged / (strength + f32(1e-06))


def on_device(momentum, mode_list):
    frame = momentum[0, 0]
    comps, grid_len = frame.shape[:2]
    frames = lax.axis_size("frames")
    blocks = lax.axis_size("tblk")
    lags = min(LAG_MAX, frames)
    mode_rows = mode_list.reshape(frames, LANES)
    tables = [y_table(grid_len), x_table(grid_len), z_table(grid_len)]
    places = [pltpu.VMEM(mode_rows.shape, jnp.int32), pltpu.SMEM(mode_rows.shape, jnp.int32)]
    lagged = pl.pallas_call(
        functools.partial(program_kernel, frames, blocks, lags),
        out_shape=jax.ShapeDtypeStruct((lags, LANES), f32),
        in_specs=[pl.BlockSpec(memory_space=pl.ANY)] * 5,
        out_specs=pl.BlockSpec(memory_space=pltpu.VMEM),
        scratch_shapes=[pltpu.VMEM(frame.shape, bf16), pltpu.VMEM(mode_rows.shape, jnp.int32)]
        + [pltpu.VMEM(table.shape, table.dtype) for table in tables]
        + [
            pltpu.VMEM((grid_len * 2 * PITCH, LANES), f32),
            pltpu.VMEM(((HALF + 1) * ROWS * CHANNELS, LANES), f32),
        ]
        + places
        + places
        + [
            pltpu.VMEM((frames, CHANNELS, LANES), f32),
            pltpu.VMEM((frames + lags, CHANNELS, LANES), f32),
            pltpu.SemaphoreType.DMA((comps, 4)),
            pltpu.SemaphoreType.DMA((4,)),
            pltpu.SemaphoreType.DMA((2,)),
            pltpu.SemaphoreType.DMA((frames,)),
            pltpu.SemaphoreType.DMA((frames,)),
            pltpu.SemaphoreType.DMA((frames + lags,)),
        ],
        compiler_params=pltpu.CompilerParams(
            collective_id=0, has_side_effects=True, vmem_limit_bytes=56 * 1024 * 1024
        ),
        name="modes_exchange_lags",
    )(frame, mode_rows, *[jnp.asarray(table) for table in tables])
    return pl.pallas_call(
        finish_kernel,
        out_shape=(
            jax.ShapeDtypeStruct((1, lags, LANES), f32),
            jax.ShapeDtypeStruct((1, LANES), f32),
        ),
        in_specs=[pl.BlockSpec(memory_space=pl.ANY)],
        scratch_shapes=[pltpu.VMEM(lagged.shape, f32), pltpu.SemaphoreType.DMA],
        compiler_params=pltpu.CompilerParams(vmem_limit_bytes=56 * 1024 * 1024),
        name="correlation",
    )(lagged)


def solution(mesh):
    placed = (P("tblk", "frames", None, None, None, None), P())
    return jax.shard_map(
        on_device,
        mesh=mesh,
        in_specs=placed,
        out_specs=(P("tblk", None, "frames"), P("tblk", "frames")),
        check_vma=False,
    )
```

```python
import functools

import jax
import jax.numpy as jnp
import ml_dtypes
import numpy as np
from jax import lax
from jax.experimental import pallas as pl
from jax.experimental.pallas import tpu as pltpu
from jax.sharding import PartitionSpec as P

KMAX = 32
LAG_MAX = 64
HALF = KMAX + 1
SIDE = 2 * KMAX + 1
PITCH = -(-HALF // 4) * 4
ROWS = -(-SIDE // 8) * 8
CHANNELS = 8
LANES = 128
LANE_BITS = 7
DIVIDE_BITS = 19

f32 = jnp.float32
bf16 = jnp.bfloat16
MESH = pl.DeviceIdType.MESH


def split_table(table):
    high = table.astype(np.float32).astype(ml_dtypes.bfloat16)
    low = (table - high.astype(np.float64)).astype(np.float32).astype(ml_dtypes.bfloat16)
    return high, low


def angles(length, frequency):
    turns = np.mod(np.outer(frequency, np.arange(length)), length)
    return turns * (2.0 * np.pi / length)


def y_table(length):
    theta = angles(length, np.arange(HALF))
    table = np.zeros((2 * PITCH, length))
    table[:HALF] = np.cos(theta)
    table[PITCH : PITCH + HALF] = np.sin(theta)
    return np.concatenate(split_table(table), axis=0)


def x_table(length):
    theta = angles(length, np.arange(-KMAX, KMAX + 1))
    table = np.zeros((2 * ROWS, 2 * length))
    table[:SIDE, :length] = np.cos(theta)
    table[:SIDE, length:] = -np.sin(theta)
    table[ROWS : ROWS + SIDE, :length] = -np.sin(theta)
    table[ROWS : ROWS + SIDE, length:] = -np.cos(theta)
    both = np.concatenate(split_table(table), axis=0)
    return np.stack([both[:, :length], both[:, length:]])


def z_table(length):
    theta = angles(length, np.arange(-KMAX, KMAX + 1))
    cos_z = np.cos(theta).astype(np.float32).astype(ml_dtypes.bfloat16).astype(np.float32)
    sin_z = (-np.sin(theta)).astype(np.float32).astype(ml_dtypes.bfloat16).astype(np.float32)
    half = CHANNELS // 2
    return np.stack([cos_z] * CHANNELS + [-sin_z] * half + [sin_z] * half, axis=1)


def by_side(value):
    return (value * (-(-(1 << DIVIDE_BITS) // SIDE))) >> DIVIDE_BITS


def decode(mode_list):
    rest = by_side(mode_list)
    z_freq = by_side(rest)
    return mode_list - rest * SIDE - KMAX, rest - z_freq * SIDE - KMAX, z_freq


def program_kernel(
    frames, blocks, lags, frame_hbm, list_hbm, ty_hbm, tx_hbm, tz_hbm, lagged_ref,
    data, mode_rows, ty_ref, tx_ref, tz_ref, along_y, plane, place_vmem, place_smem,
    freq_vmem, freq_smem, packet, held, data_sem, table_sem, place_sem,
    send_sem, late_sem, recv_sem,
):
    comps, grid_len, _, _ = frame_hbm.shape
    chunk = grid_len // data_sem.shape[1]
    chunks = grid_len // chunk
    me = lax.axis_index("frames")
    block = lax.axis_index("tblk")
    tail = lags - 1
    has_later = block < blocks - 1
    sends_back = jnp.logical_and(block > 0, me < tail)
    barrier = pltpu.get_barrier_semaphore()

    def fetch(comp, part):
        rows = pl.ds(part * chunk, chunk)
        return pltpu.make_async_copy(
            frame_hbm.at[comp, rows], data.at[comp, rows], data_sem.at[comp, part]
        )

    list_in = pltpu.make_async_copy(list_hbm, mode_rows, table_sem.at[0])
    ty_in = pltpu.make_async_copy(ty_hbm, ty_ref, table_sem.at[1])
    tx_in = pltpu.make_async_copy(tx_hbm, tx_ref, table_sem.at[2])
    tz_in = pltpu.make_async_copy(tz_hbm, tz_ref, table_sem.at[3])
    ty_in.start()
    list_in.start()
    for comp in range(comps):
        for part in range(chunks):
            fetch(comp, part).start()
            if comp == 0 and part == 0:
                tx_in.start()
    tz_in.start()

    def greet(frame, in_block):
        pl.semaphore_signal(
            barrier, inc=1, device_id={"frames": frame, "tblk": in_block}, device_id_type=MESH
        )

    @pl.loop(1, frames)
    def _(step):
        greet(lax.rem(me + step, frames), block)

    @pl.when(has_later)
    def _():
        @pl.loop(0, tail)
        def _(frame):
            greet(frame, block + 1)

    list_in.wait()
    x_freq, y_freq, z_freq = decode(mode_rows[...])
    sign = jnp.where(y_freq < 0, -1, 1)
    place_vmem[...] = sign * (y_freq * ROWS + x_freq) + KMAX
    freq_vmem[...] = sign * z_freq + KMAX
    place_out = pltpu.make_async_copy(place_vmem, place_smem, place_sem.at[0])
    freq_out = pltpu.make_async_copy(freq_vmem, freq_smem, place_sem.at[1])
    place_out.start()
    freq_out.start()

    ty_in.wait()
    tx_in.wait()
    table_y = ty_ref[...]

    @pl.loop(0, comps)
    def _(comp):
        @pl.loop(0, chunks)
        def _(part):
            fetch(comp, part).wait()
            for step in range(0, chunk, 2):
                x_at = part * chunk + step
                both = jnp.concatenate([data[comp, x_at], data[comp, x_at + 1]], axis=1)
                res = jnp.dot(table_y, both, preferred_element_type=f32)
                res = res[: 2 * PITCH] + res[2 * PITCH :]
                first = pl.multiple_of(x_at * 2 * PITCH, 8)
                along_y[pl.ds(first, 2 * PITCH), :] = res[:, :LANES]
                second = pl.multiple_of((x_at + 1) * 2 * PITCH, 8)
                along_y[pl.ds(second, 2 * PITCH), :] = res[:, LANES:]

        for ky in range(0, HALF, 2):

            def take(row):
                return along_y[pl.ds(row, grid_len, stride=2 * PITCH), :]

            cos_part = jnp.concatenate([take(ky), take(ky + 1)], axis=1)
            sin_part = jnp.concatenate([take(PITCH + ky), take(PITCH + ky + 1)], axis=1)
            values = jnp.concatenate([cos_part, sin_part], axis=0)
            high = values.astype(bf16)
            low = (values - high.astype(f32)).astype(bf16)
            table_x = jnp.concatenate([tx_ref[0], tx_ref[1]], axis=1)
            res = jnp.dot(table_x, high, preferred_element_type=f32)
            res_low = jnp.dot(table_x[: 2 * ROWS], low, preferred_element_type=f32)
            res = res[: 2 * ROWS] + res[2 * ROWS :] + res_low
            half = CHANNELS // 2
            for which in range(2):
                lanes = slice(which * LANES, (which + 1) * LANES)
                base = (ky + which) * ROWS * CHANNELS + comp
                real, imag = res[:ROWS, lanes], res[ROWS:, lanes]
                for at, value in enumerate((real, imag)):
                    plane[pl.ds(base + at * half, ROWS, stride=CHANNELS), :] = value

    place_out.wait()
    freq_out.wait()
    tz_in.wait()
    pl.semaphore_wait(barrier, frames - 1 + jnp.where(sends_back, frames, 0))

    def within(owner):
        return pltpu.make_async_remote_copy(
            src_ref=packet.at[owner],
            dst_ref=held.at[me],
            send_sem=send_sem.at[owner],
            recv_sem=recv_sem.at[me],
            device_id={"frames": owner, "tblk": block},
            device_id_type=MESH,
        )

    def backward(owner):
        return pltpu.make_async_remote_copy(
            src_ref=packet.at[owner],
            dst_ref=held.at[frames + me],
            send_sem=late_sem.at[owner],
            recv_sem=recv_sem.at[frames + me],
            device_id={"frames": owner, "tblk": block - 1},
            device_id_type=MESH,
        )

    def arrival(slot):
        return pltpu.make_async_remote_copy(
            src_ref=held.at[slot],
            dst_ref=held.at[slot],
            send_sem=send_sem.at[0],
            recv_sem=recv_sem.at[slot],
            device_id={"frames": me, "tblk": block},
            device_id_type=MESH,
        )

    lane = lax.broadcasted_iota(jnp.int32, (CHANNELS, LANES), 1)
    row = lax.broadcasted_iota(jnp.int32, (CHANNELS, LANES), 0)
    bits = [1 << level for level in range(LANE_BITS)]
    odd = [(lane & bit) != 0 for bit in bits]
    upper = row < CHANNELS // 2
    used = (row & 3) != 3
    scale = f32(float(grid_len) ** -1.5)

    def picked(owner):
        def leaf(mode):
            place = place_smem[owner, mode] * CHANNELS
            freq = freq_smem[owner, mode]
            value = plane[pl.ds(place, CHANNELS), :]
            swapped = pltpu.roll(value, CHANNELS // 2, 0)
            return value * tz_ref[freq, :CHANNELS] + swapped * tz_ref[freq, CHANNELS:]

        def tree(start, level):
            if level < 0:
                return leaf(start)
            left = tree(start, level - 1)
            right = tree(start + bits[level], level - 1)
            kept = jnp.where(odd[level], right, left)
            moved = jnp.where(odd[level], left, right)
            return kept + pltpu.roll(moved, bits[level], 1)

        total = tree(0, len(bits) - 1)
        current = jnp.where(used, total, f32(0)) * scale
        x_f, y_f, z_f = (k.astype(f32) for k in decode(mode_rows[pl.ds(owner, 1), :]))
        wave = jnp.where((row & 3) == 0, x_f, jnp.where((row & 3) == 1, y_f, z_f))
        wave_sq = x_f * x_f + y_f * y_f + z_f * z_f
        along = current * wave
        real_dot = jnp.sum(jnp.where(upper, along, f32(0)), axis=0, keepdims=True)
        imag_dot = jnp.sum(jnp.where(upper, f32(0), along), axis=0, keepdims=True)
        removed = wave * (jnp.where(upper, real_dot, imag_dot) / wave_sq)
        return current - jnp.where(used, removed, f32(0))

    @pl.loop(0, frames)
    def _(step):
        pair = [lax.rem(me + step, frames)]
        transverse = [picked(owner) for owner in pair]
        for owner, value in zip(pair, transverse):
            packet[owner] = value

        @pl.when(sends_back)
        def _():
            for owner in pair:
                backward(owner).start()

        @pl.when(step > 0)
        def _():
            within(pair[0]).start()

        @pl.when(step == 0)
        def _():
            held[me] = transverse[0]

    @pl.when(jnp.logical_not(has_later))
    def _():
        held[pl.ds(frames, lags)] = jnp.zeros((lags,) + held.shape[1:], f32)

    @pl.loop(1, frames)
    def _(step):
        arrival(lax.rem(me + step, frames)).wait_recv()

    @pl.when(has_later)
    def _():
        held[frames + tail] = jnp.zeros(held.shape[1:], f32)

        @pl.loop(0, tail)
        def _(frame):
            arrival(frames + frame).wait_recv()

    anchors = held[pl.ds(0, frames)]

    def lag_rows(first):
        for tau in range(8):
            products = jnp.sum(anchors * held[pl.ds(first + tau, frames)], axis=0)
            total = jnp.sum(products, axis=0, keepdims=True)
            lagged_ref[pl.ds(first + tau, 1), :] = total
        taus = lax.broadcasted_iota(jnp.int32, (8, LANES), 0) + first
        pairs = jnp.where(has_later, frames, frames - taus).astype(f32)
        rows = pl.ds(first, 8)
        lagged_ref[rows, :] = lagged_ref[rows, :] / pairs

    @pl.loop(0, lags, step=8)
    def _(first):
        lag_rows(pl.multiple_of(first, 8))

    @pl.loop(1, frames)
    def _(step):
        within(lax.rem(me + step, frames)).wait_send()

    @pl.when(sends_back)
    def _():
        @pl.loop(0, frames)
        def _(owner):
            backward(owner).wait_send()


def finish_kernel(lagged_hbm, corr_ref, strength_ref, lagged_ref, sem):
    lagged_in = pltpu.make_async_copy(lagged_hbm, lagged_ref, sem)
    lagged_in.start()
    lagged_in.wait()
    lagged = lagged_ref[...]
    strength = lagged[:1]
    strength_ref[...] = strength
    corr_ref[0] = lagged / (strength + f32(1e-06))


def on_device(momentum, mode_list):
    frame = momentum[0, 0]
    comps, grid_len = frame.shape[:2]
    frames = lax.axis_size("frames")
    blocks = lax.axis_size("tblk")
    lags = min(LAG_MAX, frames)
    mode_rows = mode_list.reshape(frames, LANES)
    tables = [y_table(grid_len), x_table(grid_len), z_table(grid_len)]
    places = [pltpu.VMEM(mode_rows.shape, jnp.int32), pltpu.SMEM(mode_rows.shape, jnp.int32)]
    lagged = pl.pallas_call(
        functools.partial(program_kernel, frames, blocks, lags),
        out_shape=jax.ShapeDtypeStruct((lags, LANES), f32),
        in_specs=[pl.BlockSpec(memory_space=pl.ANY)] * 5,
        out_specs=pl.BlockSpec(memory_space=pltpu.VMEM),
        scratch_shapes=[pltpu.VMEM(frame.shape, bf16), pltpu.VMEM(mode_rows.shape, jnp.int32)]
        + [pltpu.VMEM(table.shape, table.dtype) for table in tables]
        + [
            pltpu.VMEM((grid_len * 2 * PITCH, LANES), f32),
            pltpu.VMEM(((HALF + 1) * ROWS * CHANNELS, LANES), f32),
        ]
        + places
        + places
        + [
            pltpu.VMEM((frames, CHANNELS, LANES), f32),
            pltpu.VMEM((frames + lags, CHANNELS, LANES), f32),
            pltpu.SemaphoreType.DMA((comps, 4)),
            pltpu.SemaphoreType.DMA((4,)),
            pltpu.SemaphoreType.DMA((2,)),
            pltpu.SemaphoreType.DMA((frames,)),
            pltpu.SemaphoreType.DMA((frames,)),
            pltpu.SemaphoreType.DMA((frames + lags,)),
        ],
        compiler_params=pltpu.CompilerParams(
            collective_id=0, has_side_effects=True, vmem_limit_bytes=56 * 1024 * 1024
        ),
        name="modes_exchange_lags",
    )(frame, mode_rows, *[jnp.asarray(table) for table in tables])
    return pl.pallas_call(
        finish_kernel,
        out_shape=(
            jax.ShapeDtypeStruct((1, lags, LANES), f32),
            jax.ShapeDtypeStruct((1, LANES), f32),
        ),
        in_specs=[pl.BlockSpec(memory_space=pl.ANY)],
        scratch_shapes=[pltpu.VMEM(lagged.shape, f32), pltpu.SemaphoreType.DMA],
        compiler_params=pltpu.CompilerParams(vmem_limit_bytes=56 * 1024 * 1024),
        name="correlation",
    )(lagged)


def solution(mesh):
    placed = (P("tblk", "frames", None, None, None, None), P())
    return jax.shard_map(
        on_device,
        mesh=mesh,
        in_specs=placed,
        out_specs=(P("tblk", None, "frames"), P("tblk", "frames")),
        check_vma=False,
    )
```
